512 devices in a mesh: section: 2 (over core), seq: 32 (over x, z), head: 8 (over y).
Axes of the slice: x: 4, y: 8, z: 8, core: 2. Of those that a mesh axis runs over, the one named last changes fastest.
Arguments:
- prompt_states: bfloat16 [16384, 7168], P(('section', 'seq'), 'head'), may hold values from -6 to 6
- w_down: bfloat16 [7168, 576], P('head'), may hold values from -0.0625 to 0.0625
- kv_gain: float32 [512], replicated, may hold values from 0.1 to 1.9
- prompt_lengths: int32 [8], replicated, may hold values from 1 to 4096, 16384 in all
- block_owner: int32 [2048], replicated, may hold values from 0 to 31, as said below
- row_prompt: int32 [64], replicated, may hold values from 0 to 7
- queries: bfloat16 [2, 64, 128, 192], P(None, 'seq', ('section', 'head')), may hold values from -64 to 64
- new_kv: bfloat16 [2, 64, 576], P(None, 'seq'), may hold values from -64 to 64
- w_uk: bfloat16 [128, 128, 512], P(('section', 'head')), may hold values from -0.5 to 0.5
- w_uv: bfloat16 [128, 512, 128], P(('section', 'head')), may hold values from -0.25 to 0.25
Outputs:
- attended: bfloat16 [2, 64, 128, 128], P(None, 'seq', ('section', 'head'))
- decode_cache: bfloat16 [16384, 576], P('seq')
The draws below stay inside these ranges and needn't reach their ends.
Inputs may be any that keep to these rules, and one draw needn't show every extreme that they name: `block_owner`: within each aligned group of 32 blocks, the blocks of one prompt device, every seq index appears exactly 1 times.
All inputs are finite; a program needn't handle non-finite values.
Results may differ from the reference program's by a relative error of at most 0.0075.
Values may be sent and summed in bfloat16 or wider, within the bound.
A program may use at most 64 MiB of HBM per device.

```python
import math
import jax
import jax.numpy as jnp
import numpy as np
from jax import lax

D = 7168
LAT = 512
ROPE = 64
NOPE = 128
VDIM = 128
BLOCK = 8
STEPS = 2
PROMPTS = 8
BLK_PEER = 1
ROWS = 64
LATK = 576
HEADS = 128
BLOCKS_DEV = 32
TOKENS = 16384
NBLK = 2048
MOST = 4096
N_SECTION = 2
N_SEQ = 32


def shared_direction(key):
    direction = jnp.clip(jax.random.normal(key, (ROWS, ROPE), jnp.float32), -4.0, 4.0)
    chosen = jax.random.randint(jax.random.fold_in(key, 11), (ROWS,), 0, 4)
    strength = jax.random.uniform(jax.random.fold_in(key, 12), (ROWS,), jnp.float32, 5.0, 10.0)
    return (direction, jnp.where(chosen == 0, strength, 0.0))


def draw_block_owner(key, part):
    key = jax.random.fold_in(key, 5)
    group_keys = jax.random.split(key, N_SECTION * N_SEQ)
    pattern = jnp.arange(BLOCKS_DEV, dtype=jnp.int32) % N_SEQ

    def shuffle(group_key):
        return jax.random.permutation(group_key, pattern)
    return jax.vmap(shuffle)(group_keys).reshape(NBLK).astype(jnp.int32)


def draw_queries(key, part):
    direction, strength = shared_direction(key)
    key = jax.random.fold_in(key, 3)
    values = jnp.clip(jax.random.normal(key, (STEPS, ROWS, HEADS, NOPE + ROPE), jnp.float32), -6.0, 6.0)
    lift = 0.0
    rotary_extra = lift * strength[None, :, None, None] * direction[None, :, None, :]
    rotary_extra = jnp.broadcast_to(rotary_extra, (STEPS, ROWS, HEADS, ROPE))
    extra = jnp.concatenate([jnp.zeros((STEPS, ROWS, HEADS, NOPE), jnp.float32), rotary_extra], axis=-1)
    return (values + extra).astype(jnp.bfloat16)


def draw_new_kv(key, part):
    direction, strength = shared_direction(key)
    key = jax.random.fold_in(key, 7)
    values = jnp.clip(jax.random.normal(key, (STEPS, ROWS, LAT + ROPE), jnp.float32), -6.0, 6.0)
    lift = 0.0
    step_factor = 1.0 + 0.01 * jnp.arange(STEPS, dtype=jnp.float32)
    rotary_extra = lift * step_factor[:, None, None] * strength[None, :, None] * direction[None, :, :]
    extra = jnp.concatenate([jnp.zeros((STEPS, ROWS, LAT), jnp.float32), rotary_extra], axis=-1)
    return (values + extra).astype(jnp.bfloat16)


def with_ends(array, key, low, largest):
    shape = array.shape
    place = [jax.random.randint(jax.random.fold_in(key, axis), (), 0, shape[axis]) for axis in range(len(shape))]
    array = array.at[tuple(place)].set(low)
    longest = shape.index(max(shape))
    place[longest] = (place[longest] + 1) % shape[longest]
    return array.at[tuple(place)].set(largest)


def block_levels(stream_key, dims, shards, low, largest):
    def one(dim, parts):
        heights = jax.random.uniform(jax.random.fold_in(jax.random.fold_in(stream_key, 6), dim), (parts,), jnp.float32, low / len(shards), largest / len(shards))
        return jnp.repeat(jnp.exp(heights), dims[dim] // parts).reshape((-1,) + (1,) * (len(dims) - dim - 1))

    level = one(*shards[0])
    for cut in shards[1:]:
        level = level * one(*cut)
    return level


def split_up(number_of, total, reach, lean):
    loads = [(1 << 20) // math.isqrt(rank ** lean) + 1 for rank in range(2, number_of + 1)]
    surplus, given = total - reach - (number_of - 1), [1] * (number_of - 1)
    while surplus > 0:
        movable = [i for i in range(number_of - 1) if given[i] < reach]
        whole, budget = sum([loads[i] for i in movable]), surplus
        for i in movable:
            addition = min(reach - given[i], max(1, budget * loads[i] // whole), surplus)
            given[i] = given[i] + addition
            surplus = surplus - addition
    return np.array([reach] + given)


def uneven(key, amount, total, most, slope):
    if amount == 2:
        one = jax.random.randint(key, (), max(1, total - most), min(most, total - 1) + 1)
        return jnp.stack([one, total - one])
    sizes = jnp.asarray(split_up(amount, total, most, slope), jnp.int32)
    couples = (amount - 1) // 2
    source_of, receiver = sizes[1:1 + 2 * couples:2], sizes[2:2 + 2 * couples:2]
    slack = jnp.minimum(source_of - 1, most - receiver)
    moved = jax.random.randint(jax.random.fold_in(key, 1), (couples,), 0, 1 << 20) % (slack + 1)
    sizes = sizes.at[1:1 + 2 * couples:2].set(source_of - moved).at[2:2 + 2 * couples:2].set(receiver + moved)
    return sizes[jax.random.permutation(jax.random.fold_in(key, 2), amount)]


def normal_values(stream_key, dims, scale, reach, pieces=(), kind=jnp.bfloat16):
    gain = block_levels(stream_key, dims, pieces, -0.22, 0.18) if pieces else 1.0
    entries = jax.random.normal(stream_key, dims, jnp.float32) * scale * gain
    return jnp.minimum(jnp.maximum(entries, -reach), reach).astype(kind)


def setup_inputs(seed: int = 0) -> dict:
    arg_keys = jax.random.split(jax.random.key(seed), 11)
    return {
        "prompt_states": normal_values(arg_keys[0], (TOKENS, D), 1.0, 6.0, ((0, 64), (1, 8))),
        "w_down": normal_values(arg_keys[1], (D, LATK), D ** -0.5, 0.0625, ((0, 8),)),
        "kv_gain": jnp.clip(1.0 + 0.18 * jax.random.normal(arg_keys[2], (LAT,), jnp.float32), 0.1, 1.9),
        "prompt_lengths": uneven(arg_keys[3], PROMPTS, TOKENS, MOST, 2).astype(jnp.int32),
        "block_owner": draw_block_owner(jax.random.fold_in(arg_keys[10], 71), 0),
        "row_prompt": with_ends(jax.random.randint(arg_keys[5], (ROWS,), 0, PROMPTS), jax.random.fold_in(arg_keys[5], 1), 0, PROMPTS - 1).astype(jnp.int32),
        "queries": draw_queries(jax.random.fold_in(arg_keys[10], 71), 0),
        "new_kv": draw_new_kv(jax.random.fold_in(arg_keys[10], 71), 0),
        "w_uk": normal_values(arg_keys[8], (HEADS, NOPE, LAT), NOPE ** -0.5, 0.5, ((0, 16),)),
        "w_uv": normal_values(arg_keys[9], (HEADS, LAT, VDIM), LAT ** -0.5, 0.25, ((0, 16),)),
    }


def prompt_table(prompt_lengths, token_ids):
    ends = jnp.cumsum(prompt_lengths).astype(jnp.int32)
    starts = (ends - prompt_lengths).astype(jnp.int32)
    segment = lax.optimization_barrier(jnp.sum((token_ids[..., None] >= ends).astype(jnp.int32), axis=-1)).astype(jnp.int32)
    chosen = (segment[..., None] == jnp.arange(prompt_lengths.shape[0], dtype=jnp.int32)).astype(jnp.int32)
    position = (token_ids - lax.optimization_barrier(jnp.sum(chosen * starts, axis=-1))).astype(jnp.int32)
    return (segment, position)

def finish_rows(projected, kv_gain, position):
    latent_width = kv_gain.shape[0]
    latent = projected[..., :latent_width]
    rotary = projected[..., latent_width:]
    inverse = lax.rsqrt(lax.optimization_barrier(jnp.mean(latent * latent, axis=-1, keepdims=True)) + 1e-06)
    normed = latent * inverse * kv_gain
    half_width = rotary.shape[-1] // 2
    frequency = 10000.0 ** (-2.0 * jnp.arange(half_width, dtype=jnp.float32) / rotary.shape[-1])
    angle = position[..., None].astype(jnp.float32) * frequency
    cosine = jnp.cos(angle)
    sine = jnp.sin(angle)
    first_half = rotary[..., :half_width]
    second_half = rotary[..., half_width:]
    turned = jnp.concatenate([first_half * cosine - second_half * sine, second_half * cosine + first_half * sine], axis=-1)
    return jnp.concatenate([normed, turned], axis=-1)

def reference(prompt_states, w_down, kv_gain, prompt_lengths, block_owner, row_prompt, queries, new_kv, w_uk, w_uv):
    projected = jnp.dot(prompt_states, w_down, preferred_element_type=jnp.float32)
    token_ids = jnp.arange(TOKENS, dtype=jnp.int32)
    segment, position = prompt_table(prompt_lengths, token_ids)
    cache_rows = finish_rows(projected, kv_gain, position).astype(jnp.bfloat16)
    cache_rows = lax.optimization_barrier(cache_rows)
    group_count = N_SECTION * N_SEQ
    sorted_blocks = jnp.argsort(block_owner.reshape(group_count, BLOCKS_DEV), axis=1, stable=True).astype(jnp.int32)
    sorted_blocks = sorted_blocks.reshape(group_count, N_SEQ, BLK_PEER)
    block_ids = jnp.arange(group_count, dtype=jnp.int32)[:, None, None] * BLOCKS_DEV + sorted_blocks
    block_ids = block_ids.reshape(N_SECTION, N_SEQ, N_SEQ, BLK_PEER).transpose(2, 1, 3, 0)
    slot_ids = (block_ids[..., None] * BLOCK + jnp.arange(BLOCK, dtype=jnp.int32)).reshape(TOKENS)
    decode_cache = cache_rows[slot_ids]
    absorbed = jnp.einsum('srhn,hnl->srhl', queries[..., :NOPE].astype(jnp.float32), w_uk.astype(jnp.float32))
    absorbed = lax.optimization_barrier(absorbed.astype(jnp.bfloat16))
    full_query = jnp.concatenate([absorbed, queries[..., NOPE:]], axis=-1).astype(jnp.float32)
    ends = jnp.cumsum(prompt_lengths).astype(jnp.int32)
    starts = (ends - prompt_lengths).astype(jnp.int32)
    first_key = jnp.minimum(starts[row_prompt], TOKENS - MOST).astype(jnp.int32)
    cache_float = cache_rows.astype(jnp.float32)
    new_float = new_kv.astype(jnp.float32)
    up_float = w_uv.astype(jnp.float32)
    score_scale = 1.0 / math.sqrt(NOPE + ROPE)
    causal = jnp.arange(STEPS)[:, None] >= jnp.arange(STEPS)[None, :]

    def one_row(row_item):
        row_query, row_new, key_start, prompt = row_item
        window = lax.dynamic_slice_in_dim(cache_float, key_start, MOST, 0)
        window_segment = lax.dynamic_slice_in_dim(segment, key_start, MOST, 0)
        scores = jnp.einsum('shk,tk->sht', row_query, window) * score_scale
        scores = jnp.where((window_segment == prompt)[None, None, :], scores, -jnp.inf)
        own_scores = jnp.einsum('shk,uk->shu', row_query, row_new) * score_scale
        own_scores = jnp.where(causal[:, None, :], own_scores, -jnp.inf)
        row_top = jnp.maximum(lax.optimization_barrier(jnp.max(scores, axis=-1)), lax.optimization_barrier(jnp.max(own_scores, axis=-1)))
        weights = jnp.exp(scores - row_top[..., None])
        own_weights = jnp.exp(own_scores - row_top[..., None])
        denominator = lax.optimization_barrier(jnp.sum(weights, axis=-1)) + lax.optimization_barrier(jnp.sum(own_weights, axis=-1))
        probs = lax.optimization_barrier(weights.astype(jnp.bfloat16)).astype(jnp.float32)
        own_probs = lax.optimization_barrier(own_weights.astype(jnp.bfloat16)).astype(jnp.float32)
        weighted = jnp.einsum('sht,tl->shl', probs, window[:, :LAT])
        weighted = weighted + jnp.einsum('shu,ul->shl', own_probs, row_new[:, :LAT])
        context = weighted / denominator[..., None]
        lifted = jnp.einsum('shl,hlv->shv', context, up_float, precision=lax.Precision.HIGHEST)
        return lifted.astype(jnp.bfloat16)
    attended = lax.map(one_row, (full_query.transpose(1, 0, 2, 3), new_float.transpose(1, 0, 2), first_key, row_prompt))
    return (attended.transpose(1, 0, 2, 3), decode_cache)
```

```python
import functools
import math

import jax
import jax.numpy as jnp
import numpy as np
from jax import lax
from jax.experimental import pallas as pl
from jax.experimental.pallas import tpu as pltpu
from jax.sharding import PartitionSpec as P

MESH = pl.DeviceIdType.MESH
BLOCK = 8
LANES = 128
MASKED = -1e30
LOWEST = -1e25
TINY = 1e-30
F32 = jnp.float32
BF16 = jnp.bfloat16


def contract_last(a, b):
    return lax.dot_general(a, b, (((1,), (1,)), ((), ())), preferred_element_type=F32)


def matmul(a, b):
    return jnp.dot(a, b, preferred_element_type=F32)


def iota(shape, dim):
    return lax.broadcasted_iota(jnp.int32, shape, dim)


def kernel(
    n_seq,
    n_head,
    lengths,
    row_prompt,
    owner,
    states,
    w_down,
    gain,
    frequency,
    queries,
    new_kv,
    w_uk,
    w_uv,
    attended,
    cache,
    part_f32,
    part_out,
    part_in,
    keys,
    query_all,
    nope_f32,
    rope_f32,
    query_full,
    new_keys,
    cache_out,
    out_f32,
    out_send,
    out_recv,
    stat_send,
    stat_recv,
    share,
    query_send_sem,
    query_recv_sem,
    part_send_sem,
    part_recv_sem,
    key_send_sem,
    key_recv_sem,
    pass_send_sem,
    pass_recv_sem,
    cache_send_sem,
    cache_recv_sem,
    half_send_sem,
    half_recv_sem,
    out_send_sem,
    out_recv_sem,
    stat_send_sem,
    stat_recv_sem,
):
    section = lax.axis_index("section")
    me = lax.axis_index("seq")
    head = lax.axis_index("head")
    prompts = lengths.shape[0]
    tokens = states.shape[0]
    chunk = tokens // n_head
    latent = gain.shape[1]
    own_queries = queries.shape[0]
    heads = w_uk.shape[0]
    nope = w_uk.shape[1]
    rope = queries.shape[1] - nope
    width = latent + LANES
    pairs = own_queries // heads
    rows = n_seq * pairs
    scale = 1.0 / math.sqrt(nope + rope)

    def seq_peer(step):
        return lax.rem(me + step, n_seq)

    def seq_back(step):
        return lax.rem(me + n_seq - step, n_seq)

    def head_peer(step):
        return lax.rem(head + step, n_head)

    def head_back(step):
        return lax.rem(head + n_head - step, n_head)

    barrier = pltpu.get_barrier_semaphore()

    @pl.loop(1, n_seq)
    def _(step):
        pl.semaphore_signal(
            barrier, inc=1, device_id=(section, seq_peer(step), head), device_id_type=MESH
        )

    @pl.loop(1, n_head)
    def _(step):
        pl.semaphore_signal(
            barrier, inc=1, device_id=(section, me, head_peer(step)), device_id_type=MESH
        )

    pl.semaphore_signal(barrier, inc=1, device_id=(1 - section, me, head), device_id_type=MESH)

    lane = iota((own_queries, LANES), 1)
    row = iota((own_queries, LANES), 0)
    second_row = lax.rem(row // heads, 2) == 1
    prompt = jnp.where(second_row, row_prompt[2 * me + 1], row_prompt[2 * me])
    query_all[0, :, nope:] = jnp.where(lane == rope + prompt, 1.0, 0.0).astype(BF16)
    query_all[0, :, : nope + rope] = queries[...]

    part = matmul(states[...], w_down[...])
    part_f32[:, : latent + rope] = part
    part_out[:, :, latent:] = jnp.zeros((n_head, chunk, LANES), BF16)
    part_out[:, :, : latent + rope] = part.astype(BF16).reshape(n_head, chunk, latent + rope)

    pl.semaphore_wait(barrier, n_seq + n_head - 1)

    @pl.loop(1, n_head)
    def _(step):
        peer = head_peer(step)
        pltpu.make_async_remote_copy(
            src_ref=part_out.at[peer],
            dst_ref=part_in.at[step - 1],
            send_sem=part_send_sem,
            recv_sem=part_recv_sem,
            device_id=(section, me, peer),
            device_id_type=MESH,
        ).start()

    @pl.loop(1, n_seq)
    def _(step):
        pltpu.make_async_remote_copy(
            src_ref=query_all.at[0],
            dst_ref=query_all.at[step],
            send_sem=query_send_sem,
            recv_sem=query_recv_sem,
            device_id=(section, seq_peer(step), head),
            device_id_type=MESH,
        ).start()

    token = (section * n_seq + me) * tokens + head * chunk + iota((chunk, LANES), 0)
    key_lane = iota((chunk, LANES), 1)
    begin = jnp.zeros((chunk, LANES), jnp.int32)
    lane_begin = jnp.zeros((chunk, LANES), jnp.int32)
    lane_end = jnp.full((chunk, LANES), 2**30, jnp.int32)
    start = jnp.int32(0)
    for p in range(prompts):
        end = start + lengths[p]
        begin = jnp.where(token >= end, end, begin)
        lane_begin = jnp.where(key_lane == rope + p, start, lane_begin)
        lane_end = jnp.where(key_lane == rope + p, end, lane_end)
        start = end
    prompt_columns = jnp.where((token >= lane_begin) & (token < lane_end), 0.0, MASKED)
    angle = (token - begin).astype(F32) * frequency[...]
    cosine = jnp.cos(angle)
    sine = jnp.sin(angle)
    signed_sine = jnp.where(key_lane < rope // 2, -sine, sine)

    new_keys[...] = jnp.zeros(new_keys.shape, BF16)
    new_keys[: new_kv.shape[0], : latent + rope] = new_kv[...]
    own_nope = queries[:, :nope].astype(F32)
    own_head = lax.rem(iota((own_queries, nope), 0), heads)
    spread = jnp.concatenate(
        [jnp.where(own_head == h, own_nope, 0.0).astype(BF16) for h in range(heads)], axis=1
    )
    own_absorbed = matmul(spread, w_uk[...].reshape(heads * nope, latent)).astype(BF16)
    own_full = jnp.concatenate([own_absorbed, query_all[0, :, nope:]], axis=1)
    own_scores = contract_last(own_full, new_keys[...]) * scale
    column = iota(own_scores.shape, 1)
    own_row = iota(own_scores.shape, 0)
    own_allowed = (
        (column < new_kv.shape[0])
        & (lax.rem(column, 2) == lax.rem(own_row // heads, 2))
        & (column // 2 <= own_row // (2 * heads))
    )
    own_scores = jnp.where(own_allowed, own_scores, MASKED)
    own_top = jnp.max(own_scores, axis=1, keepdims=True)
    own_weights = jnp.exp(own_scores - own_top)
    own_sum = jnp.sum(own_weights, axis=1, keepdims=True)
    own_context = matmul(own_weights.astype(BF16), new_keys[:, :latent]) / own_sum
    own_context = own_context.astype(BF16)
    out_head = lax.rem(iota((own_queries, LANES), 0), heads)
    own_out = jnp.zeros((own_queries, LANES), F32)
    for h in range(heads):
        own_out = jnp.where(out_head == h, matmul(own_context, w_uv[h]), own_out)

    pltpu.make_async_copy(part_in, part_in, part_recv_sem).wait()
    total = part_f32[pl.ds(pl.multiple_of(head * chunk, chunk), chunk), :]
    for k in range(n_head - 1):
        total = total + part_in[k].astype(F32)
    low = total[:, :latent]
    inverse = lax.rsqrt(jnp.mean(low * low, axis=1, keepdims=True) + 1e-06)
    keys[section, head, :, :latent] = (low * inverse * gain[...]).astype(BF16)
    tail = total[:, latent:]
    half = rope // 2
    swapped = jnp.where(
        key_lane < half, pltpu.roll(tail, LANES - half, 1), pltpu.roll(tail, half, 1)
    )
    turned = tail * cosine + swapped * signed_sine
    keys[section, head, :, latent:] = jnp.where(key_lane < rope, turned, prompt_columns).astype(
        BF16
    )

    @pl.loop(1, n_head)
    def _(step):
        pltpu.make_async_remote_copy(
            src_ref=keys.at[section, head],
            dst_ref=keys.at[section, head],
            send_sem=key_send_sem,
            recv_sem=key_recv_sem.at[step],
            device_id=(section, me, head_peer(step)),
            device_id_type=MESH,
        ).start()

    def pass_on(step):
        source = head_back(step)
        return pltpu.make_async_remote_copy(
            src_ref=keys.at[section, source],
            dst_ref=keys.at[section, source],
            send_sem=pass_send_sem,
            recv_sem=pass_recv_sem.at[step],
            device_id=(1 - section, me, head),
            device_id_type=MESH,
        )

    pass_on(0).start()

    pltpu.make_async_copy(
        query_all.at[pl.ds(1, n_seq - 1)], query_all.at[pl.ds(1, n_seq - 1)], query_recv_sem
    ).wait()
    for part_ref, lanes in ((nope_f32, slice(0, nope)), (rope_f32, slice(nope, None))):
        part_ref[...] = query_all[:, :, lanes].astype(F32).reshape(part_ref.shape)
    for h in range(heads):
        query = nope_f32[pl.ds(h, rows, stride=heads), :].astype(BF16)
        query_full[h, :, :latent] = matmul(query, w_uk[h]).astype(BF16)
        query_full[h, :, latent:] = rope_f32[pl.ds(h, rows, stride=heads), :].astype(BF16)

    for step in range(1, n_head):
        source = head_back(step)
        pltpu.make_async_copy(
            keys.at[section, source], keys.at[section, source], key_recv_sem.at[step]
        ).wait()
        pass_on(step).start()
    for step in range(n_head):
        source = head_back(step)
        pltpu.make_async_copy(
            keys.at[1 - section, source], keys.at[1 - section, source], pass_recv_sem.at[step]
        ).wait()

    all_keys = keys[...].reshape(2 * tokens, width)
    picks = []
    for s in range(2):
        owners = owner[pl.ds(s * n_seq + me, 1), :].astype(F32)
        owners = jnp.broadcast_to(owners, (16, owners.shape[1])).astype(BF16)
        expand = (
            iota((owners.shape[1], tokens), 1) // BLOCK == iota((owners.shape[1], tokens), 0)
        )
        owners = matmul(owners, jnp.where(expand, 1.0, 0.0).astype(BF16))[:1]
        slot = iota((2 * tokens, tokens), 0)
        wanted = (slot // (2 * BLOCK)).astype(F32)
        same_place = lax.rem(slot, 2 * BLOCK) == s * BLOCK + lax.rem(
            iota((2 * tokens, tokens), 1), BLOCK
        )
        picks.append(jnp.where((owners == wanted) & same_place, 1.0, 0.0).astype(BF16))
    ordered = matmul(jnp.concatenate(picks, axis=1), all_keys)
    cache_out[...] = ordered[:, : latent + rope].astype(BF16).reshape(cache_out.shape)

    half_seq = n_seq // 2
    two = 2 * BLOCK
    my_half = lax.rem(section + me // half_seq, 2)
    my_rows = pl.ds(pl.multiple_of(me * two, two), two)

    @pl.loop(0, half_seq)
    def _(step):
        peer = my_half * half_seq + lax.rem(me + step, half_seq)

        @pl.when(peer != me)
        def _():
            pltpu.make_async_remote_copy(
                src_ref=cache_out.at[peer],
                dst_ref=cache.at[my_rows],
                send_sem=cache_send_sem,
                recv_sem=cache_recv_sem,
                device_id=(section, peer, head),
                device_id_type=MESH,
            ).start()

        @pl.when(peer == me)
        def _():
            pltpu.make_async_copy(cache_out.at[me], cache.at[my_rows], cache_recv_sem).start()

    stat_lane = iota((rows, LANES), 1)
    stats = jnp.zeros((rows, LANES), F32)
    for h in range(heads):
        scores = contract_last(query_full[h], all_keys) * scale
        top = jnp.maximum(jnp.max(scores, axis=1, keepdims=True), LOWEST)
        weights = jnp.exp(scores - top)
        weight_sum = jnp.maximum(jnp.sum(weights, axis=1, keepdims=True), TINY)
        context = matmul(weights.astype(BF16), all_keys[:, :latent])
        out = matmul(context.astype(BF16), w_uv[h]) / weight_sum
        out_f32[pl.ds(h, rows, stride=heads), :] = out
        stats = jnp.where(stat_lane == h, top, stats)
        stats = jnp.where(stat_lane == heads + h, weight_sum, stats)
    stat_send[...] = stats.reshape(stat_send.shape)
    out_send[...] = out_f32[...].astype(BF16).reshape(out_send.shape)

    @pl.loop(1, n_seq)
    def _(step):
        target = (section, seq_back(step), head)
        pltpu.make_async_remote_copy(
            src_ref=stat_send.at[step],
            dst_ref=stat_recv.at[step],
            send_sem=stat_send_sem,
            recv_sem=stat_recv_sem,
            device_id=target,
            device_id_type=MESH,
        ).start()
        pltpu.make_async_remote_copy(
            src_ref=out_send.at[step],
            dst_ref=out_recv.at[step],
            send_sem=out_send_sem,
            recv_sem=out_recv_sem,
            device_id=target,
            device_id_type=MESH,
        ).start()

    stat_recv[0] = stat_send[0]
    out_recv[0] = out_send[0]

    half_rows = half_seq * two
    half_ref = cache.at[pl.ds(pl.multiple_of(my_half * half_rows, half_rows), half_rows)]
    pltpu.make_async_copy(half_ref, half_ref, cache_recv_sem).wait()
    pass_half = pltpu.make_async_remote_copy(
        src_ref=half_ref,
        dst_ref=half_ref,
        send_sem=half_send_sem,
        recv_sem=half_recv_sem,
        device_id=(1 - section, me, head),
        device_id_type=MESH,
    )
    pass_half.start()

    others = pl.ds(1, n_seq - 1)
    pltpu.make_async_copy(stat_recv.at[others], stat_recv.at[others], stat_recv_sem).wait()
    diagonal = iota((pairs, heads, LANES), 1) == iota((pairs, heads, LANES), 2)

    def compact(column):
        return jnp.sum(jnp.where(diagonal, column.reshape(pairs, heads, 1), 0.0), axis=1)

    compact_top = compact(own_top)
    compact_sum = compact(own_sum)
    tops = stat_recv[...]
    sums = pltpu.roll(tops.reshape(n_seq * pairs, LANES), LANES - heads, 1).reshape(tops.shape)
    best = jnp.maximum(jnp.max(tops, axis=0), compact_top)
    shares = jnp.exp(tops - best) * sums
    own_share = jnp.exp(compact_top - best) * compact_sum
    norm = 1.0 / (jnp.sum(shares, axis=0) + own_share)
    share[...] = shares * norm

    def expand(compacted):
        picked = jnp.where(diagonal, compacted.reshape(pairs, 1, LANES), 0.0)
        return jnp.sum(picked, axis=2, keepdims=True)

    result = expand(own_share * norm) * own_out.reshape(pairs, heads, LANES)
    pltpu.make_async_copy(out_recv.at[others], out_recv.at[others], out_recv_sem).wait()
    for step in range(n_seq):
        piece = out_recv[step].astype(F32).reshape(pairs, heads, LANES)
        result = result + expand(share[step]) * piece
    attended[...] = result.reshape(own_queries, LANES).astype(BF16)

    pltpu.make_async_copy(part_in, part_in, part_send_sem).wait()
    pltpu.make_async_copy(query_all.at[others], query_all.at[others], query_send_sem).wait()
    others_head = keys.at[section, pl.ds(0, n_head - 1)]
    pltpu.make_async_copy(others_head, others_head, key_send_sem).wait()
    pltpu.make_async_copy(keys.at[section], keys.at[section], pass_send_sem).wait()
    pltpu.make_async_copy(stat_recv.at[others], stat_recv.at[others], stat_send_sem).wait()
    pltpu.make_async_copy(out_recv.at[others], out_recv.at[others], out_send_sem).wait()
    sent = cache_out.at[pl.ds(0, half_seq - 1)]
    pltpu.make_async_copy(sent, sent, cache_send_sem).wait()

    @pl.when(my_half != me // half_seq)
    def _():
        pltpu.make_async_copy(cache_out.at[0], cache_out.at[0], cache_send_sem).wait()

    pass_half.wait_send()
    other = cache.at[pl.ds(pl.multiple_of((1 - my_half) * half_rows, half_rows), half_rows)]
    pltpu.make_async_copy(other, other, half_recv_sem).wait()


def solution(mesh):
    n_seq = mesh.shape["seq"]
    n_head = mesh.shape["head"]

    def on_device(
        prompt_states,
        w_down,
        kv_gain,
        prompt_lengths,
        block_owner,
        row_prompt,
        queries,
        new_kv,
        w_uk,
        w_uv,
    ):
        tokens = prompt_states.shape[0]
        steps, own_rows, heads, query_width = queries.shape
        latent = kv_gain.shape[0]
        total = w_down.shape[1]
        rope = total - latent
        pairs = steps * own_rows
        own_queries = pairs * heads
        width = latent + LANES
        chunk = tokens // n_head
        value = w_uv.shape[2]
        exponent = np.arange(rope // 2, dtype=np.float64)
        frequency = np.zeros((1, LANES), np.float32)
        frequency[0, :rope] = np.tile(10000.0 ** (-2.0 * exponent / rope), 2)
        vmem = pl.BlockSpec(memory_space=pltpu.VMEM)
        smem = pl.BlockSpec(memory_space=pltpu.SMEM)
        dma = pltpu.SemaphoreType.DMA
        attended, cache = pl.pallas_call(
            functools.partial(kernel, n_seq, n_head),
            out_shape=(
                jax.ShapeDtypeStruct((own_queries, value), BF16),
                jax.ShapeDtypeStruct((2 * tokens, total), BF16),
            ),
            in_specs=[smem, smem] + [vmem] * 9,
            out_specs=(vmem, pl.BlockSpec(memory_space=pl.ANY)),
            scratch_shapes=[
                pltpu.VMEM((tokens, width), F32),
                pltpu.VMEM((n_head, chunk, width), BF16),
                pltpu.VMEM((n_head - 1, chunk, width), BF16),
                pltpu.VMEM((2, n_head, chunk, width), BF16),
                pltpu.VMEM((n_seq, own_queries, 2 * LANES), BF16),
                pltpu.VMEM((n_seq * own_queries, LANES), F32),
                pltpu.VMEM((n_seq * own_queries, LANES), F32),
                pltpu.VMEM((heads, n_seq * pairs, width), BF16),
                pltpu.VMEM((LANES, width), BF16),
                pltpu.VMEM((n_seq, 2 * BLOCK, total), BF16),
                pltpu.VMEM((n_seq * own_queries, value), F32),
                pltpu.VMEM((n_seq, own_queries, value), BF16),
                pltpu.VMEM((n_seq, own_queries, value), BF16),
                pltpu.VMEM((n_seq, pairs, LANES), F32),
                pltpu.VMEM((n_seq, pairs, LANES), F32),
                pltpu.VMEM((n_seq, pairs, LANES), F32),
                dma,
                dma,
                dma,
                dma,
                dma,
                dma((n_head,)),
                dma,
                dma((n_head,)),
                dma,
                dma,
                dma,
                dma,
                dma,
                dma,
                dma,
                dma,
            ],
            compiler_params=pltpu.CompilerParams(
                collective_id=0, has_side_effects=True, vmem_limit_bytes=48 * 2**20
            ),
        )(
            prompt_lengths,
            row_prompt,
            block_owner.reshape(2 * n_seq, -1),
            prompt_states,
            w_down,
            kv_gain.reshape(1, latent),
            jnp.asarray(frequency),
            queries.reshape(own_queries, query_width),
            new_kv.reshape(pairs, total),
            w_uk,
            w_uv,
        )
        return (attended.reshape(steps, own_rows, heads, value), cache)

    placed = (
        P(("section", "seq"), "head"),
        P("head", None),
        P(),
        P(),
        P(),
        P(),
        P(None, "seq", ("section", "head"), None),
        P(None, "seq", None),
        P(("section", "head"), None, None),
        P(("section", "head"), None, None),
    )
    return jax.shard_map(
        on_device,
        mesh=mesh,
        in_specs=placed,
        out_specs=(P(None, "seq", ("section", "head"), None), P("seq", None)),
        check_vma=False,
    )
```
